128 devices in a mesh: row: 32 (over z, y, core), grp: 4 (over x).
Axes of the slice: x: 4, y: 4, z: 4, core: 2. Of those that a mesh axis runs over, the one named last changes fastest.
Arguments:
- tiles: float32 [2048, 20, 128, 128], P(('row', 'grp')), may hold values from 0.01 to 1
- tile_cols: int32 [2048, 20], P(('row', 'grp')), may hold values from 0 to 2047, as said below
- tile_counts: int32 [2048], P(('row', 'grp')), may hold values from 8 to 20, as said below
- block: float32 [262144, 128], P(('row', 'grp')), may hold values from -6 to 6
Outputs:
- next_block: float32 [262144, 128], P(('row', 'grp'))
The draws below stay inside these ranges and needn't reach their ends.
Inputs may be any that keep to these rules, and one draw needn't show every extreme that they name: `tile_counts`: every tile-row has at least 8 live tiles and every device has a tile-row with all 20 live. `tile_cols`: device p (in the order of row then grp) owns tile-columns p * 16 to (p + 1) * 16 - 1. For every ordered pair of different devices, exactly 1 live tiles of the first refer to tile-columns owned by the second; every other slot, live or not, refers to a tile-column of its own device.
All inputs are finite; a program needn't handle non-finite values.
Results may differ from the reference program's by a relative error of at most 0.0003.
Values sent between devices are 32-bit elements; how exact they have to be, the bound alone decides.
A program may use at most 192 MiB of HBM per device.

```python
import math
import jax
import jax.numpy as jnp
from jax import lax

TILE = 128
VECS = 128
TILE_ROWS_DEV = 16
REMOTE = 1
ITERS = 2
MAXT = 20
LIVE_MIN = 8
TILE_ROWS = 2048
NROWS = 262144


def counts_shared(key):
    devices_all = TILE_ROWS // TILE_ROWS_DEV
    heavy = jax.random.randint(jax.random.fold_in(key, 11), (devices_all, 1), 0, 4)
    spread = MAXT - LIVE_MIN
    raw_counts = jax.random.randint(jax.random.fold_in(key, 12), (devices_all, TILE_ROWS_DEV), 0, spread + 1)
    counts = LIVE_MIN + jnp.minimum(spread, raw_counts * (1 + heavy) // 3)
    full_row = jax.random.randint(jax.random.fold_in(key, 13), (devices_all, 1), 0, TILE_ROWS_DEV)
    counts = jnp.where(jnp.arange(TILE_ROWS_DEV)[None, :] == full_row, MAXT, counts)
    return counts.astype(jnp.int32)


def draw_tile_counts(key, part):
    counts = counts_shared(key)
    return counts.reshape(TILE_ROWS).astype(jnp.int32)


def draw_tile_cols(key, part):
    counts = counts_shared(key)
    key = jax.random.fold_in(key, 5)
    devices_all = TILE_ROWS // TILE_ROWS_DEV
    slot_total = TILE_ROWS_DEV * MAXT
    remote_total = (devices_all - 1) * REMOTE
    live_mask = (jnp.arange(MAXT)[None, None, :] < counts[:, :, None]).reshape(devices_all, slot_total).astype(jnp.int32)
    noise = jax.random.randint(jax.random.fold_in(key, 1), (devices_all, slot_total), 0, 2 ** 20)
    score = noise * slot_total + jnp.arange(slot_total, dtype=jnp.int32)[None, :] + live_mask * 2 ** 30
    order = jnp.argsort(-score, axis=1)
    chosen = order[:, :remote_total]
    device_ids = jnp.arange(devices_all, dtype=jnp.int32)[:, None]
    peers = (device_ids + 1 + jnp.arange(remote_total, dtype=jnp.int32)[None, :] % (devices_all - 1)) % devices_all
    owners = jnp.broadcast_to(device_ids, (devices_all, slot_total))
    owners = owners.at[device_ids, chosen].set(peers)
    local_ids = jax.random.randint(jax.random.fold_in(key, 2), (devices_all, slot_total), 0, TILE_ROWS_DEV)
    return (owners * TILE_ROWS_DEV + local_ids).reshape(TILE_ROWS, MAXT).astype(jnp.int32)


def block_levels(rng, dims, shards, low, top_value):
    loudness = 1.0
    for position, parts in shards:
        steps = jax.random.uniform(jax.random.fold_in(jax.random.fold_in(rng, 6), position), (parts,), jnp.float32, low / len(shards), top_value / len(shards))
        loudness = loudness * jnp.repeat(jnp.exp(steps), dims[position] // parts).reshape((-1,) + (1,) * (len(dims) - 1 - position))
    return loudness


def scatter_about(stream_key, dims, deviation, reach, split=(), kind=jnp.bfloat16):
    factor_of = block_levels(stream_key, dims, split, -0.22, 0.18) if split else 1.0
    array = jax.random.normal(stream_key, dims, jnp.float32) * deviation * factor_of
    return jnp.minimum(jnp.maximum(array, -reach), reach).astype(kind)


def setup_inputs(seed: int = 0) -> dict:
    key_list = jax.random.split(jax.random.key(seed), 5)
    return {
        "tiles": jnp.clip(jnp.exp(math.log(1.0) - 4.6051702 * jax.random.uniform(key_list[0], (TILE_ROWS, MAXT, TILE, TILE), jnp.float32) ** block_levels(key_list[0], (TILE_ROWS, MAXT, TILE, TILE), ((0, 128),), -0.2, 0.2)), 0.01, 1.0),
        "tile_cols": draw_tile_cols(jax.random.fold_in(key_list[4], 71), 0),
        "tile_counts": draw_tile_counts(jax.random.fold_in(key_list[4], 71), 0),
        "block": scatter_about(key_list[3], (NROWS, VECS), 1.0, 6.0, ((0, 128),), jnp.float32),
    }


def reference(tiles, tile_cols, tile_counts, block):
    live_mask = (jnp.arange(MAXT)[None, :] < tile_counts[:, None]).astype(jnp.float32)
    degree = jnp.einsum('rsij,rs->ri', tiles, live_mask, precision=lax.Precision.HIGHEST)
    inv_root = 1.0 / jnp.sqrt(degree)
    current = block
    for sweep_no in range(ITERS):
        scaled = current.reshape(TILE_ROWS, TILE, VECS) * inv_root[:, :, None]

        def one_row(pieces):
            row_tiles, row_cols, row_live = pieces
            gathered = scaled[row_cols]
            return jnp.einsum('sij,sjk,s->ik', row_tiles, gathered, row_live, precision=lax.Precision.HIGHEST)
        summed = lax.map(one_row, (tiles, tile_cols, live_mask))
        image = (summed * inv_root[:, :, None]).reshape(NROWS, VECS)
        gram_sum = jnp.dot(image.T.astype(jnp.float32), image.astype(jnp.float32), precision=lax.Precision.HIGHEST, preferred_element_type=jnp.float32)
        factor = jnp.linalg.cholesky(gram_sum)
        current = lax.linalg.triangular_solve(factor, image, left_side=False, lower=True, transpose_a=True) * jnp.sqrt(jnp.float32(NROWS))
    return current
```

```python
import functools

import jax
import jax.numpy as jnp
from jax import lax
from jax.experimental import pallas as pl
from jax.experimental.pallas import tpu as pltpu
from jax.sharding import PartitionSpec as P

MESH = pl.DeviceIdType.MESH
T = 128
ROWS = 16
SLOTS = 20
ITERS = 2
PARTS = (48, 40, 40)
STARTS = (0, 48, 88)
ORDERS = (("z", "x", "y"), ("y", "z", "x"), ("x", "y", "z"))
STEPS = (1, 3, 2)
HIGH = lax.Precision.HIGHEST
F32 = jnp.float32


def split(a):
    hi = a.astype(jnp.bfloat16)
    return hi, (a - hi.astype(F32)).astype(jnp.bfloat16)


def product(a, b):
    ah, al = split(a)
    bh, bl = split(b)
    dot = functools.partial(jnp.dot, preferred_element_type=F32)
    return dot(ah, bh) + (dot(ah, bl) + dot(al, bh))


def inverse_factor(m_ref, v_ref):
    lane = lax.broadcasted_iota(jnp.int32, (8, T), 1)
    sub = lax.broadcasted_iota(jnp.int32, (8, T), 0)
    v_ref[...] = (
        lax.broadcasted_iota(jnp.int32, (T, T), 0) == lax.broadcasted_iota(jnp.int32, (T, T), 1)
    ).astype(F32)

    def block(b, carry):
        base = pl.multiple_of(b * 8, 8)
        p = m_ref[pl.ds(base, 8), :]
        q = v_ref[pl.ds(base, 8), :]
        for j in range(8):
            col = jnp.sum(jnp.where(lane == base + j, p, 0.0), axis=1, keepdims=True)
            scale = 1.0 / jnp.sqrt(col[j : j + 1, :])
            prow = p[j : j + 1, :] * scale
            qrow = q[j : j + 1, :] * scale
            coef = jnp.where(sub > j, col * scale, 0.0)
            p = jnp.where(sub == j, prow, p - coef * prow)
            q = jnp.where(sub == j, qrow, q - coef * qrow)
        v_ref[pl.ds(base, 8), :] = q
        below = jnp.where(lane >= base + 8, p, 0.0)
        both = jnp.concatenate([p, q], axis=1)
        update = lax.dot_general(
            below, both, (((0,), (0,)), ((), ())), precision=HIGH, preferred_element_type=F32
        )
        m_ref[...] -= update[:, :T]
        v_ref[...] -= update[:, T:]
        return carry

    lax.fori_loop(0, T // 8, block, 0)


def kernel(
    tiles_hbm, block_ref, want_ref, slot_ref, own_ref, far_ref, live_ref, out_ref,
    tiles, ag0, ag1, ag2, ag3, ag4, ag5, ag6, ag7, ag8, ag9, ag10, ag11, st0, st1, st2, xr0, xr1, xr2, fn0, fn1, fn2,
    scaled, acc, inv, sums, gram, factor, wtab, stab,
    load_sem, s1s, s1r, s2s, s2r, s3s, s3r, loc_sem, ws, wr, tab_sem, gs, gr, free_in, free_out,
):
    ag = ((ag0, ag1, ag2, ag3), (ag4, ag5, ag6, ag7), (ag8, ag9, ag10, ag11))
    st, xr, fn = (st0, st1, st2), (xr0, xr1, xr2), (fn0, fn1, fn2)
    row, grp = lax.axis_index("row"), lax.axis_index("grp")
    at = {"z": row // 8, "y": (row // 2) % 4, "x": grp, "c": row % 2}

    def device(**by):
        v = {k: lax.rem(at[k] + by[k], 2 if k == "c" else 4) if k in by else at[k] for k in at}
        return (v["z"] * 8 + v["y"] * 2 + v["c"], v["x"])

    for r in range(ROWS):
        pltpu.make_async_copy(tiles_hbm.at[r], tiles.at[r], load_sem.at[r]).start()

    barrier = pltpu.get_barrier_semaphore()
    same_core = [{a: d} for a in "xyz" for d in STEPS]
    all_peers = same_core + [{a: d, "c": 1} for a in "xyz" for d in STEPS] + [{"c": 1}]
    for by in all_peers:
        pl.semaphore_signal(barrier, inc=1, device_id=device(**by), device_id_type=MESH)
    pl.semaphore_wait(barrier, len(all_peers))

    wtab[0, 0, 0, 0] = want_ref[...]

    def table_copies(stage):
        axis = "zyxc"[stage]
        copies = []
        for d in (1,) if axis == "c" else STEPS:
            src, dst = {
                "z": (wtab.at[0, 0, 0, 0], wtab.at[0, 0, 0, d]),
                "y": (wtab.at[0, 0, 0], wtab.at[0, 0, d]),
                "x": (wtab.at[0, 0], wtab.at[0, d]),
                "c": (wtab.at[0], wtab.at[d]),
            }[axis]
            copies.append(
                pltpu.make_async_remote_copy(
                    src, dst, ws.at[stage, d], wr.at[stage, d], device_id=device(**{axis: d}), device_id_type=MESH
                )
            )
        return copies

    def degree_row(r):
        pltpu.make_async_copy(tiles_hbm.at[r], tiles.at[r], load_sem.at[r]).wait()

        def add(s, total):
            return total + tiles[r, s] * live_ref[r * SLOTS + s]

        total = lax.fori_loop(0, SLOTS, add, jnp.zeros((T, T), F32), unroll=4)
        root = 1.0 / jnp.sqrt(jnp.sum(total, axis=1, keepdims=True))
        inv[r] = jnp.broadcast_to(root, (T, T))

    for stage in range(4):
        copies = table_copies(stage)
        for copy in copies:
            copy.start()

        def some(r, carry):
            degree_row(r)
            return carry

        lax.fori_loop(stage * 4, stage * 4 + 4, some, 0)
        for copy in copies:
            copy.wait()
    table = pltpu.make_async_copy(wtab, stab, tab_sem)
    table.start()

    scaled[ROWS] = jnp.zeros((T, T), F32)
    for i in range(3):
        fn[i][0, 0] = jnp.zeros((PARTS[i], T), F32)

    def put(r, value):
        scaled[r] = value
        for i in range(3):
            ag[i][0][r] = value[STARTS[i] : STARTS[i] + PARTS[i], :]

    def begin(r, carry):
        put(r, block_ref[r] * inv[r])
        return carry

    lax.fori_loop(0, ROWS, begin, 0)
    table.wait()

    def gather_copy(i, d):
        return pltpu.make_async_remote_copy(
            ag[i][0], ag[i][d], s1s.at[i, d], s1r.at[i, d],
            device_id=device(**{ORDERS[i][0]: d}), device_id_type=MESH,
        )

    def second_copy(i, d2, d1):
        return pltpu.make_async_remote_copy(
            st[i].at[d2 - 1, d1], xr[i].at[d2, d1], s2s.at[i, d2, d1], s2r.at[i, d2, d1],
            device_id=device(**{ORDERS[i][1]: d2}), device_id_type=MESH,
        )

    def select(i, d1):
        a1, a2, a3 = ORDERS[i]
        for d2 in range(4):

            def pick(e, carry):
                d3, dc = e // 2, e % 2
                off = {a1: d1, a2: d2, a3: d3}
                back = {a1: 0, a2: (4 - d2) % 4, a3: lax.rem(4 - d3, 4)}
                place = ((off["x"] * 4 + off["y"]) * 4 + off["z"]) * 2 + dc
                which = stab[dc, back["x"], back["y"], back["z"], 0, place]
                value = ag[i][d1][which]
                if d2 == 0:
                    xr[i][0, d1, e] = value
                else:
                    st[i][d2 - 1, d1, e] = value
                return carry

            lax.fori_loop(0, 8, pick, 0, unroll=4)

    def third_start(i, d2):
        a3 = ORDERS[i][2]
        for e in (2, 6, 3, 7, 4, 5, 1):
            by = {a3: e // 2} if e >= 2 else {}
            if e % 2:
                by["c"] = 1
            pltpu.make_async_remote_copy(
                xr[i].at[d2, :, e], fn[i].at[e, pl.ds(d2 * 4, 4)], s3s.at[i], s3r.at[i],
                device_id=device(**by), device_id_type=MESH,
            ).start()

    def third_all(i):
        return pltpu.make_async_remote_copy(
            fn[i].at[pl.ds(1, 7)], fn[i].at[pl.ds(1, 7)], s3s.at[i], s3r.at[i],
            device_id=device(c=1), device_id_type=MESH,
        )

    def own_copy(i, d2):
        first = 1 if d2 == 0 else 0
        return pltpu.make_async_copy(
            xr[i].at[d2, pl.ds(first, 4 - first), 0],
            fn[i].at[0, pl.ds(d2 * 4 + first, 4 - first)],
            loc_sem.at[i, d2],
        )

    def home(r, carry):
        total = jnp.zeros((T, T), F32)
        for s in range(0, SLOTS, 2):
            a = jnp.concatenate([tiles[r, s], tiles[r, s + 1]], axis=1)
            b = jnp.concatenate([scaled[own_ref[r * SLOTS + s]], scaled[own_ref[r * SLOTS + s + 1]]], axis=0)
            total = total + product(a, b)
        acc[r] = total
        return carry

    def far_places(dx, dy, dz, dc):
        off = {"x": dx, "y": dy, "z": dz}
        return [(off[a3] * 2 + dc, off[a2] * 4 + off[a1]) for a1, a2, a3 in ORDERS]

    def far_products(first, group, carry):
        for lower in range(first, 8):
            places = far_places(group // 4, group % 4, lower // 2, lower % 2)
            slot = slot_ref[group * 8 + lower]
            x = jnp.concatenate([fn[i][places[i]] for i in range(3)], axis=0)
            value = product(tiles[slot // SLOTS, lax.rem(slot, SLOTS)], x)
            for i in range(3):
                fn[i][places[i]] = value[STARTS[i] : STARTS[i] + PARTS[i], :]
        return carry

    def add_far(r):
        total = acc[r]
        pieces = [total[STARTS[i] : STARTS[i] + PARTS[i], :] for i in range(3)]
        for s in range(SLOTS):
            for i in range(3):
                where = far_ref[i, r * SLOTS + s]
                pieces[i] = pieces[i] + fn[i][where // 16, lax.rem(where, 16)]
        return jnp.concatenate(pieces, axis=0) * inv[r]

    def gram_copies(it, stage):
        axis = "cxyz"[stage]
        return [
            pltpu.make_async_remote_copy(
                sums.at[it, stage, 0], sums.at[it, stage, d], gs.at[it, stage, d], gr.at[it, stage, d],
                device_id=device(**{axis: d}), device_id_type=MESH,
            )
            for d in ((1,) if axis == "c" else STEPS)
        ]

    def gram_start(it, stage):
        sums[it, stage, 0] = gram[...]
        for copy in gram_copies(it, stage):
            copy.start()

    def gram_finish(it, stage):
        copies = gram_copies(it, stage)
        for copy in copies:
            copy.wait()
        for d in range(1, len(copies) + 1):
            gram[...] += sums[it, stage, d]

    def local_gram():
        def add(r, total):
            a = acc[r]
            return total + lax.dot_general(
                a, a, (((0,), (0,)), ((), ())), precision=HIGH, preferred_element_type=F32
            )

        gram[...] = lax.fori_loop(0, ROWS, add, jnp.zeros((T, T), F32))

    root_total = jnp.sqrt(F32(ROWS * T * 128))

    def normalised(value):
        return root_total * lax.dot_general(
            value, factor[...], (((1,), (1,)), ((), ())), precision=HIGH, preferred_element_type=F32
        )

    for it in range(ITERS):
        if it:
            pl.semaphore_wait(free_in, len(same_core))
        for d in STEPS:
            for i in range(3):
                gather_copy(i, d).start()
        if it:
            local_gram()
            gram_start(0, 0)
        for d1 in (0, *STEPS):
            for i in range(3):
                if d1:
                    gather_copy(i, d1).wait_recv()
                select(i, d1)
                for d2 in STEPS:
                    second_copy(i, d2, d1).start()
            if it:
                stage = (0, *STEPS).index(d1)
                gram_finish(0, stage)
                if stage < 3:
                    gram_start(0, stage + 1)
        if it:
            pl.semaphore_wait(free_out, len(all_peers))
        for i in range(3):
            third_start(i, 0)
            own_copy(i, 0).start()
        lax.fori_loop(0, ROWS, home, 0)
        if it:
            inverse_factor(gram, factor)
        for d2 in STEPS:
            for i in range(3):
                for d1 in range(4):
                    second_copy(i, d2, d1).wait_recv()
                third_start(i, d2)
                own_copy(i, d2).start()
        for i in range(3):
            for d in STEPS:
                gather_copy(i, d).wait_send()
                for d1 in range(4):
                    second_copy(i, d, d1).wait_send()
            third_all(i).wait_send()
            for d2 in range(4):
                own_copy(i, d2).wait()
        if it == 0:
            for by in same_core:
                pl.semaphore_signal(free_in, inc=1, device_id=device(**by), device_id_type=MESH)
        for i in range(3):
            third_all(i).wait_recv()
        far_products(1, 0, 0)
        lax.fori_loop(1, 16, functools.partial(far_products, 0), 0)

        if it == 0:

            def close(r, carry):
                image = add_far(r)
                acc[r] = image
                put(r, image * inv[r])
                return carry

            lax.fori_loop(0, ROWS, close, 0)
            for by in all_peers:
                pl.semaphore_signal(free_out, inc=1, device_id=device(**by), device_id_type=MESH)
        else:

            def close_last(r, carry):
                acc[r] = normalised(add_far(r))
                return carry

            lax.fori_loop(0, ROWS, close_last, 0)
    local_gram()
    for stage in range(4):
        gram_start(1, stage)
        gram_finish(1, stage)
    inverse_factor(gram, factor)

    def finish(r, carry):
        out_ref[r] = normalised(acc[r])
        return carry

    lax.fori_loop(0, ROWS, finish, 0)


def per_device(tiles, tile_cols, tile_counts, block):
    row, grp = lax.axis_index("row"), lax.axis_index("grp")
    me = {"z": row // 8, "y": (row // 2) % 4, "c": row % 2, "x": grp}
    slot = jnp.arange(ROWS * SLOTS, dtype=jnp.int32)
    cols = tile_cols.reshape(ROWS * SLOTS)
    owner, local = cols // ROWS, cols % ROWS
    live = (jnp.arange(SLOTS)[None, :] < tile_counts[:, None]).reshape(ROWS * SLOTS)
    away = {
        "x": (me["x"] - owner) % 4,
        "c": (me["c"] - owner // 4) % 2,
        "y": (me["y"] - owner // 8) % 4,
        "z": (me["z"] - owner // 32) % 4,
    }
    place = ((away["x"] * 4 + away["y"]) * 4 + away["z"]) * 2 + away["c"]
    far = place > 0
    hot = (place[:, None] == jnp.arange(128)[None, :]) & far[:, None]
    want = jnp.sum(jnp.where(hot, local[:, None], 0), axis=0).reshape(1, 128)
    far_slot = jnp.sum(jnp.where(hot, slot[:, None], 0), axis=0)
    own = jnp.where(live & ~far, local, ROWS)
    far_place = jnp.stack(
        [
            jnp.where(far, ((away[a3] * 2 + away["c"]) * 4 + away[a2]) * 4 + away[a1], 0)
            for a1, a2, a3 in ORDERS
        ]
    )
    smem, vmem = pl.BlockSpec(memory_space=pltpu.SMEM), pl.BlockSpec(memory_space=pltpu.VMEM)
    dma = pltpu.SemaphoreType.DMA
    out = pl.pallas_call(
        kernel,
        out_shape=jax.ShapeDtypeStruct((ROWS, T, T), F32),
        in_specs=[pl.BlockSpec(memory_space=pl.ANY), vmem, vmem, smem, smem, smem, smem],
        out_specs=vmem,
        scratch_shapes=[
            pltpu.VMEM((ROWS, SLOTS, T, T), F32),
            *[pltpu.VMEM((ROWS, n, T), F32) for n in PARTS for _ in range(4)],
            *[pltpu.VMEM((3, 4, 8, n, T), F32) for n in PARTS],
            *[pltpu.VMEM((4, 4, 8, n, T), F32) for n in PARTS],
            *[pltpu.VMEM((8, 16, n, T), F32) for n in PARTS],
            pltpu.VMEM((ROWS + 1, T, T), F32),
            pltpu.VMEM((ROWS, T, T), F32),
            pltpu.VMEM((ROWS, T, T), F32),
            pltpu.VMEM((2, 4, 4, T, T), F32),
            pltpu.VMEM((T, T), F32),
            pltpu.VMEM((T, T), F32),
            pltpu.VMEM((2, 4, 4, 4, 1, T), jnp.int32),
            pltpu.SMEM((2, 4, 4, 4, 1, T), jnp.int32),
            dma((ROWS,)),
            dma((3, 4)),
            dma((3, 4)),
            dma((3, 4, 4)),
            dma((3, 4, 4)),
            dma((3,)),
            dma((3,)),
            dma((3, 4)),
            dma((4, 4)),
            dma((4, 4)),
            dma,
            dma((2, 4, 4)),
            dma((2, 4, 4)),
            pltpu.SemaphoreType.REGULAR,
            pltpu.SemaphoreType.REGULAR,
        ],
        compiler_params=pltpu.CompilerParams(
            collective_id=0, has_side_effects=True, vmem_limit_bytes=60 * 2**20
        ),
    )(
        tiles, block.reshape(ROWS, T, T), want.astype(jnp.int32), far_slot.astype(jnp.int32),
        own.astype(jnp.int32), far_place.astype(jnp.int32), live.astype(F32),
    )
    return out.reshape(ROWS * T, T)


def solution(mesh):
    shard = ("row", "grp")
    return jax.shard_map(
        per_device,
        mesh=mesh,
        in_specs=(P(shard, None, None, None), P(shard, None), P(shard), P(shard, None)),
        out_specs=P(shard, None),
        check_vma=False,
    )
```

```python
import functools

import jax
import jax.numpy as jnp
from jax import lax
from jax.experimental import pallas as pl
from jax.experimental.pallas import tpu as pltpu
from jax.sharding import PartitionSpec as P

MESH = pl.DeviceIdType.MESH
T = 128
ROWS = 16
SLOTS = 20
ITERS = 2
PARTS = (48, 40, 40)
STARTS = (0, 48, 88)
ORDERS = (("z", "x", "y"), ("y", "z", "x"), ("x", "y", "z"))
STEPS = (1, 3, 2)
FAR_STEP = 8
STAGED = 6
HIGH = lax.Precision.HIGHEST
F32 = jnp.float32


def split(a):
    hi = a.astype(jnp.bfloat16)
    return hi, (a - hi.astype(F32)).astype(jnp.bfloat16)


def inverse_factor(m_ref, v_ref):
    lane = lax.broadcasted_iota(jnp.int32, (8, T), 1)
    sub = lax.broadcasted_iota(jnp.int32, (8, T), 0)
    v_ref[...] = (
        lax.broadcasted_iota(jnp.int32, (T, T), 0) == lax.broadcasted_iota(jnp.int32, (T, T), 1)
    ).astype(F32)

    def block(b, carry):
        base = pl.multiple_of(b * 8, 8)
        p = m_ref[pl.ds(base, 8), :]
        q = v_ref[pl.ds(base, 8), :]
        cols = [
            jnp.broadcast_to(jnp.sum(jnp.where(lane == base + j, p, 0.0), axis=1, keepdims=True), (8, T))
            for j in range(8)
        ]
        for j in range(8):
            pivot = jnp.broadcast_to(cols[j][j : j + 1, :], (8, T))
            scale = lax.rsqrt(pivot)
            scale = scale * (1.5 - 0.5 * pivot * scale * scale)
            coef = jnp.where(sub > j, cols[j] * scale, 0.0)
            for m in range(j + 1, 8):
                cols[m] = cols[m] - coef * (jnp.broadcast_to(cols[m][j : j + 1, :], (8, T)) * scale)
            prow = jnp.broadcast_to(p[j : j + 1, :], (8, T)) * scale
            qrow = jnp.broadcast_to(q[j : j + 1, :], (8, T)) * scale
            p = jnp.where(sub == j, prow, p - coef * prow)
            q = jnp.where(sub == j, qrow, q - coef * qrow)
        v_ref[pl.ds(base, 8), :] = q
        below = jnp.where(lane >= base + 8, p, 0.0)
        both = jnp.concatenate([p, q], axis=1)
        update = lax.dot_general(
            below, both, (((0,), (0,)), ((), ())), precision=HIGH, preferred_element_type=F32
        )
        m_ref[...] -= update[:, :T]
        v_ref[...] -= update[:, T:]
        return carry

    lax.fori_loop(0, T // 8, block, 0)


def index_kernel(cols_ref, counts_ref, want_ref, own_ref, slot_ref, place_ref, keep_ref, last_ref):
    row, x = lax.axis_index("row"), lax.axis_index("grp")
    z, y, c = row // 8, (row // 2) % 4, row % 2
    want_ref[0, 0] = 0
    slot_ref[127] = 0
    keep_ref[127] = 0
    for i in range(3):
        place_ref[i, 127] = 0

    def one_row(r, first):
        last_ref[r] = 127
        count = counts_ref[r]

        def one_slot(s, n):
            col = cols_ref[r, s]
            owner, local = col >> 4, col & 15
            away = {"x": (x - owner) & 3, "y": (y - (owner >> 3)) & 3, "z": (z - (owner >> 5)) & 3}
            dc = (c - (owner >> 2)) & 1
            place = away["x"] * 32 + away["y"] * 8 + away["z"] * 2 + dc
            far = place != 0
            k = r * SLOTS + s
            own_ref[k] = jnp.where(far | (s >= count), ROWS, local)

            @pl.when(far)
            def _():
                want_ref[0, place] = local
                slot_ref[n] = k
                for i, (a1, a2, a3) in enumerate(ORDERS):
                    place_ref[i, n] = (away[a3] * 2 + dc) * 16 + away[a2] * 4 + away[a1]
                keep_ref[n] = jnp.where(n == first, 0, 1)
                last_ref[r] = n

            return n + far.astype(jnp.int32)

        return lax.fori_loop(0, SLOTS, one_slot, first)

    lax.fori_loop(0, ROWS, one_row, jnp.int32(0))


def kernel(
    tiles_hbm, block_ref, want_ref, own_ref, slot_ref, place_ref, keep_ref, last_ref, counts_ref, out_ref,
    whi, wlo, work, ag1, ag2, ag3, ag4, ag5, ag6, ag7, ag8, ag9,
    st0, st1, st2, xr0, xr1, xr2, fn0, fn1, fn2, xs, xcat, inv, icol, ic0, ic1, ic2,
    gsrc, gpart, gline, gout, factor, wtab, stab,
    load_sem, s1s, s1r, fs, fr, is_, ir, s2s, s2r, s3s, s3r, loc_sem, ws, wr, tab_sem, gs, gr, free_in, free_out,
):
    ag = ((None, ag1, ag2, ag3), (None, ag4, ag5, ag6), (None, ag7, ag8, ag9))
    st, xr, fn, ic = (st0, st1, st2), (xr0, xr1, xr2), (fn0, fn1, fn2), (ic0, ic1, ic2)
    acc = out_ref
    row, grp = lax.axis_index("row"), lax.axis_index("grp")
    at = {"z": row // 8, "y": (row // 2) % 4, "x": grp, "c": row % 2}

    def device(**by):
        v = {k: lax.rem(at[k] + by[k], 2 if k == "c" else 4) if k in by else at[k] for k in at}
        return (v["z"] * 8 + v["y"] * 2 + v["c"], v["x"])

    def load_copy(r):
        place = pl.multiple_of(lax.rem(r, STAGED) * SLOTS, SLOTS)
        return pltpu.make_async_copy(tiles_hbm.at[r], work.at[pl.ds(place, SLOTS)], load_sem.at[r])

    for r in range(STAGED):
        load_copy(r).start()

    barrier = pltpu.get_barrier_semaphore()
    same_core = [{a: d} for a in "xyz" for d in STEPS]
    all_peers = same_core + [{a: d, "c": 1} for a in "xyz" for d in STEPS] + [{"c": 1}]
    for by in all_peers:
        pl.semaphore_signal(barrier, inc=1, device_id=device(**by), device_id_type=MESH)
    pl.semaphore_wait(barrier, len(all_peers))

    def gather_copy(i, d, it):
        source = xs if it else block_ref
        return pltpu.make_async_remote_copy(
            source.at[:, pl.ds(STARTS[i], PARTS[i])], ag[i][d], s1s.at[i, d], s1r.at[i, d],
            device_id=device(**{ORDERS[i][0]: d}), device_id_type=MESH,
        )

    half = ROWS // 2

    def forward_copy(i, d):
        part = pl.ds(0 if d == 1 else half, half)
        return pltpu.make_async_remote_copy(
            ag[i][d].at[part], ag[i][2].at[part], fs.at[i, d], fr.at[i, d],
            device_id=device(**{ORDERS[i][0]: d}), device_id_type=MESH,
        )

    def root_copy(i, d):
        return pltpu.make_async_remote_copy(
            icol.at[pl.ds(STARTS[i], PARTS[i])], ic[i].at[d], is_.at[i, d], ir.at[i, d],
            device_id=device(**{ORDERS[i][0]: d}), device_id_type=MESH,
        )

    wtab[0, 0, 0, 0] = want_ref[...]

    def table_copies(stage):
        axis = "zyxc"[stage]
        copies = []
        for d in (1,) if axis == "c" else STEPS:
            src, dst = {
                "z": (wtab.at[0, 0, 0, 0], wtab.at[0, 0, 0, d]),
                "y": (wtab.at[0, 0, 0], wtab.at[0, 0, d]),
                "x": (wtab.at[0, 0], wtab.at[0, d]),
                "c": (wtab.at[0], wtab.at[d]),
            }[axis]
            copies.append(
                pltpu.make_async_remote_copy(
                    src, dst, ws.at[stage, d], wr.at[stage, d], device_id=device(**{axis: d}), device_id_type=MESH
                )
            )
        return copies

    lane = lax.broadcasted_iota(jnp.int32, (T, T), 1)

    def take_row(r, columns):
        load_copy(r).wait()
        place = lax.rem(r, STAGED) * SLOTS
        count = counts_ref[r]

        def add(s, total):
            tile = work[place + s]
            hi, lo = split(tile)
            whi[r, s] = hi
            wlo[r, s] = lo
            return total + tile * jnp.where(s < count, 1.0, 0.0)

        total = lax.fori_loop(0, SLOTS, add, jnp.zeros((T, T), F32), unroll=4)
        root = 1.0 / jnp.sqrt(jnp.sum(total, axis=1, keepdims=True))
        inv[r] = jnp.broadcast_to(root, (T, T))
        return jnp.where(lane == r, root, columns)

    def take_and_load(r, columns):
        columns = take_row(r, columns)
        load_copy(r + STAGED).start()
        return columns

    columns = jnp.zeros((T, T), F32)
    for stage in range(4):
        copies = table_copies(stage)
        for copy in copies:
            copy.start()
        if stage == 0:
            for d in (1, 3):
                for i in range(3):
                    gather_copy(i, d, 0).start()
        low, high = stage * 4, stage * 4 + 4
        middle = min(max(ROWS - STAGED, low), high)
        columns = lax.fori_loop(low, middle, take_and_load, columns)
        columns = lax.fori_loop(middle, high, take_row, columns)
        for copy in copies:
            copy.wait()
    icol[...] = columns
    for d in STEPS:
        for i in range(3):
            root_copy(i, d).start()
    table = pltpu.make_async_copy(wtab, stab, tab_sem)
    table.start()

    xcat[ROWS] = jnp.zeros((T, 2 * T), jnp.bfloat16)
    for i in range(3):
        fn[i][0, 0] = jnp.zeros((PARTS[i], T), F32)

    def put(r, value):
        xs[r] = value
        xcat[r] = jnp.concatenate(split(value), axis=1)

    def begin(r, carry):
        put(r, block_ref[r] * inv[r])
        return carry

    lax.fori_loop(0, ROWS, begin, 0)
    table.wait()

    def second_copy(i, d2, d1):
        return pltpu.make_async_remote_copy(
            st[i].at[d2 - 1, d1], xr[i].at[d2, d1], s2s.at[i, d2, d1], s2r.at[i, d2, d1],
            device_id=device(**{ORDERS[i][1]: d2}), device_id_type=MESH,
        )

    def select(i, d1, it):
        a1, a2, a3 = ORDERS[i]
        for d2 in range(4):

            def pick(e, carry):
                d3, dc = e // 2, e % 2
                off = {a1: d1, a2: d2, a3: d3}
                back = {a1: 0, a2: (4 - d2) % 4, a3: lax.rem(4 - d3, 4)}
                place = ((off["x"] * 4 + off["y"]) * 4 + off["z"]) * 2 + dc
                which = stab[dc, back["x"], back["y"], back["z"], 0, place]
                if d1 == 0:
                    value = xs[which, STARTS[i] : STARTS[i] + PARTS[i]]
                else:
                    value = ag[i][d1][which]
                if d1 and it == 0:
                    roots = jnp.where(lane[: PARTS[i]] == which, ic[i][d1], 0.0)
                    value = value * jnp.sum(roots, axis=1, keepdims=True)
                if d2 == 0:
                    xr[i][0, d1, e] = value
                else:
                    st[i][d2 - 1, d1, e] = value
                return carry

            lax.fori_loop(0, 8, pick, 0, unroll=4)

    def third_start(i, d2):
        a3 = ORDERS[i][2]
        for e in (2, 6, 3, 7, 4, 5, 1):
            by = {a3: e // 2} if e >= 2 else {}
            if e % 2:
                by["c"] = 1
            pltpu.make_async_remote_copy(
                xr[i].at[d2, :, e], fn[i].at[e, pl.ds(d2 * 4, 4)], s3s.at[i], s3r.at[i],
                device_id=device(**by), device_id_type=MESH,
            ).start()

    def third_all(i):
        return pltpu.make_async_remote_copy(
            fn[i].at[pl.ds(1, 7)], fn[i].at[pl.ds(1, 7)], s3s.at[i], s3r.at[i],
            device_id=device(c=1), device_id_type=MESH,
        )

    def own_copy(i, d2):
        first = 1 if d2 == 0 else 0
        return pltpu.make_async_copy(
            xr[i].at[d2, pl.ds(first, 4 - first), 0],
            fn[i].at[0, pl.ds(d2 * 4 + first, 4 - first)],
            loc_sem.at[i, d2],
        )

    dot = functools.partial(jnp.dot, preferred_element_type=F32)

    def home(r, carry):
        total = jnp.zeros((T, 2 * T), F32)
        small = jnp.zeros((T, T), F32)
        for s in range(0, SLOTS, 2):
            b = jnp.concatenate([xcat[own_ref[r * SLOTS + s]], xcat[own_ref[r * SLOTS + s + 1]]], axis=0)
            total = total + dot(jnp.concatenate([whi[r, s], whi[r, s + 1]], axis=1), b)
            small = small + dot(jnp.concatenate([wlo[r, s], wlo[r, s + 1]], axis=1), b[:, :T])
        acc[r] = total[:, :T] + (total[:, T:] + small)
        return carry

    def far_products(group, running):
        values = []
        for k in range(FAR_STEP):
            k = group * FAR_STEP + k
            slot = slot_ref[k]
            pieces = []
            for i in range(3):
                where = place_ref[i, k]
                pieces.append(fn[i][where // 16, lax.rem(where, 16)])
            hi, lo = split(jnp.concatenate(pieces, axis=0))
            r, s = slot // SLOTS, lax.rem(slot, SLOTS)
            wide = dot(whi[r, s], jnp.concatenate([hi, lo], axis=1))
            values.append(wide[:, :T] + (wide[:, T:] + dot(wlo[r, s], hi)))
        for k in range(FAR_STEP):
            running = jnp.where(keep_ref[group * FAR_STEP + k] > 0, running, 0.0) + values[k]
            work[group * FAR_STEP + k] = running
        return running

    def add_far(r):
        return (acc[r] + work[last_ref[r]]) * inv[r]

    group = [(dx, dc) for dx in range(4) for dc in range(2) if dx or dc]
    mine = pl.multiple_of((at["x"] * 2 + at["c"]) * 16, 16)

    def gram_copies(it, stage):
        copies = []
        if stage in (1, 2):
            axis = "yz"[stage - 1]
            for d in STEPS:
                copies.append(
                    pltpu.make_async_remote_copy(
                        gline.at[it, stage - 1, 0], gline.at[it, stage - 1, d],
                        gs.at[it, stage, d], gr.at[it, stage, d],
                        device_id=device(**{axis: d}), device_id_type=MESH,
                    )
                )
            return copies
        for dx, dc in group:
            by = {k: v for k, v in (("x", dx), ("c", dc)) if v}
            e = dx * 2 + dc
            if stage == 0:
                theirs = lax.rem(at["x"] + dx, 4) * 2 + lax.rem(at["c"] + dc, 2)
                src, dst = gsrc.at[it, pl.ds(pl.multiple_of(theirs * 16, 16), 16)], gpart.at[it, e]
            else:
                src = dst = gout.at[it, pl.ds(mine, 16)]
            copies.append(
                pltpu.make_async_remote_copy(
                    src, dst, gs.at[it, stage, e], gr.at[it, stage, e], device_id=device(**by), device_id_type=MESH
                )
            )
        return copies

    def gram_start(it, stage):
        for copy in gram_copies(it, stage):
            copy.start()

    def gram_finish(it, stage):
        for copy in gram_copies(it, stage):
            copy.wait()
        if stage == 0:
            total = gsrc[it, pl.ds(mine, 16)]
            for dx, dc in group:
                total = total + gpart[it, dx * 2 + dc]
        elif stage < 3:
            total = (gline[it, stage - 1, 0] + gline[it, stage - 1, 1]) + (gline[it, stage - 1, 2] + gline[it, stage - 1, 3])
        if stage < 2:
            gline[it, stage, 0] = total
        elif stage == 2:
            gout[it, pl.ds(mine, 16)] = total

    def local_gram(it):
        def add(r, total):
            a = acc[r]
            return total + lax.dot_general(
                a, a, (((0,), (0,)), ((), ())), precision=HIGH, preferred_element_type=F32
            )

        gsrc[it] = lax.fori_loop(0, ROWS, add, jnp.zeros((T, T), F32))

    root_total = jnp.sqrt(F32(ROWS * T * 128))

    def normalised(value):
        return root_total * lax.dot_general(
            value, factor[...], (((1,), (1,)), ((), ())), precision=HIGH, preferred_element_type=F32
        )

    for it in range(ITERS):

        def forward_start():
            for d in (1, 3):
                for i in range(3):
                    gather_copy(i, d, it).wait_recv()
                    forward_copy(i, d).start()

        def second_start(d1s, d2s):
            for d2 in d2s:
                for d1 in d1s:
                    for i in range(3):
                        second_copy(i, d2, d1).start()

        if it:
            pl.semaphore_wait(free_in, len(same_core))
            for d in (1, 3):
                for i in range(3):
                    gather_copy(i, d, it).start()
        else:
            forward_start()
        for i in range(3):
            select(i, 0, it)
        second_start((0,), (1, 3, 2))
        if it:
            local_gram(0)
            gram_start(0, 0)
            lax.fori_loop(0, 5, home, 0)
            gram_finish(0, 0)
            gram_start(0, 1)
            forward_start()
        else:
            for d in STEPS:
                for i in range(3):
                    root_copy(i, d).wait_recv()
        for d in (1, 3):
            for i in range(3):
                select(i, d, it)
        second_start((1, 3), (2, 1, 3))
        if it:
            gram_finish(0, 1)
            gram_start(0, 2)
            lax.fori_loop(5, 9, home, 0)
        for i in range(3):
            for d in (1, 3):
                forward_copy(i, d).wait_recv()
            select(i, 2, it)
        second_start((2,), (2, 1, 3))
        if it:
            pl.semaphore_wait(free_out, len(all_peers))
        for i in range(3):
            third_start(i, 0)
            own_copy(i, 0).start()
        if it:
            gram_finish(0, 2)
            gram_start(0, 3)
        lax.fori_loop(9 if it else 0, ROWS, home, 0)
        for d2 in (2, 1, 3):
            for i in (1, 2, 0):
                for d1 in range(4):
                    second_copy(i, d2, d1).wait_recv()
                third_start(i, d2)
                own_copy(i, d2).start()
        if it:
            gram_finish(0, 3)
            inverse_factor(gout.at[0], factor)
        for i in range(3):
            for d in (1, 3):
                gather_copy(i, d, it).wait_send()
                forward_copy(i, d).wait_send()
            for d in STEPS:
                if it == 0:
                    root_copy(i, d).wait_send()
                for d1 in range(4):
                    second_copy(i, d, d1).wait_send()
            third_all(i).wait_send()
            for d2 in range(4):
                own_copy(i, d2).wait()
        if it == 0:
            for by in same_core:
                pl.semaphore_signal(free_in, inc=1, device_id=device(**by), device_id_type=MESH)
        for i in range(3):
            third_all(i).wait_recv()
        lax.fori_loop(0, 128 // FAR_STEP, far_products, jnp.zeros((T, T), F32))

        if it == 0:
            for by in all_peers:
                pl.semaphore_signal(free_out, inc=1, device_id=device(**by), device_id_type=MESH)

            def close(r, carry):
                image = add_far(r)
                acc[r] = image
                put(r, image * inv[r])
                return carry

            lax.fori_loop(0, ROWS, close, 0)
        else:

            def close_last(r, carry):
                acc[r] = normalised(add_far(r))
                return carry

            lax.fori_loop(0, ROWS, close_last, 0)
    local_gram(1)
    for stage in range(4):
        gram_start(1, stage)
        gram_finish(1, stage)
    inverse_factor(gout.at[1], factor)

    def finish(r, carry):
        out_ref[r] = normalised(acc[r])
        return carry

    lax.fori_loop(0, ROWS, finish, 0)


def per_device(tiles, tile_cols, tile_counts, block):
    smem, vmem = pl.BlockSpec(memory_space=pltpu.SMEM), pl.BlockSpec(memory_space=pltpu.VMEM)
    dma = pltpu.SemaphoreType.DMA
    ints = lambda *shape: jax.ShapeDtypeStruct(shape, jnp.int32)
    want, own, slot, place, keep, last = pl.pallas_call(
        index_kernel,
        out_shape=[ints(1, 128), ints(ROWS * SLOTS), ints(128), ints(3, 128), ints(128), ints(ROWS)],
        in_specs=[smem, smem],
        out_specs=[smem] * 6,
    )(tile_cols, tile_counts)
    out = pl.pallas_call(
        kernel,
        out_shape=jax.ShapeDtypeStruct((ROWS, T, T), F32),
        in_specs=[pl.BlockSpec(memory_space=pl.ANY), vmem, vmem] + [smem] * 6,
        out_specs=vmem,
        scratch_shapes=[
            pltpu.VMEM((ROWS, SLOTS, T, T), jnp.bfloat16),
            pltpu.VMEM((ROWS, SLOTS, T, T), jnp.bfloat16),
            pltpu.VMEM((128, T, T), F32),
            *[pltpu.VMEM((ROWS, n, T), F32) for n in PARTS for _ in range(3)],
            *[pltpu.VMEM((3, 4, 8, n, T), F32) for n in PARTS],
            *[pltpu.VMEM((4, 4, 8, n, T), F32) for n in PARTS],
            *[pltpu.VMEM((8, 16, n, T), F32) for n in PARTS],
            pltpu.VMEM((ROWS, T, T), F32),
            pltpu.VMEM((ROWS + 1, T, 2 * T), jnp.bfloat16),
            pltpu.VMEM((ROWS, T, T), F32),
            pltpu.VMEM((T, T), F32),
            *[pltpu.VMEM((4, n, T), F32) for n in PARTS],
            pltpu.VMEM((2, T, T), F32),
            pltpu.VMEM((2, 8, 16, T), F32),
            pltpu.VMEM((2, 2, 4, 16, T), F32),
            pltpu.VMEM((2, T, T), F32),
            pltpu.VMEM((T, T), F32),
            pltpu.VMEM((2, 4, 4, 4, 1, T), jnp.int32),
            pltpu.SMEM((2, 4, 4, 4, 1, T), jnp.int32),
            dma((ROWS,)),
            *[dma((3, 4)) for _ in range(6)],
            dma((3, 4, 4)),
            dma((3, 4, 4)),
            dma((3,)),
            dma((3,)),
            dma((3, 4)),
            dma((4, 4)),
            dma((4, 4)),
            dma,
            dma((2, 4, 8)),
            dma((2, 4, 8)),
            pltpu.SemaphoreType.REGULAR,
            pltpu.SemaphoreType.REGULAR,
        ],
        compiler_params=pltpu.CompilerParams(
            collective_id=0, has_side_effects=True, vmem_limit_bytes=63 * 2**20
        ),
    )(tiles, block.reshape(ROWS, T, T), want, own, slot, place, keep, last, tile_counts)
    return out.reshape(ROWS * T, T)


def solution(mesh):
    shard = ("row", "grp")
    return jax.shard_map(
        per_device,
        mesh=mesh,
        in_specs=(P(shard, None, None, None), P(shard, None), P(shard), P(shard, None)),
        out_specs=P(shard, None),
        check_vma=False,
    )
```

```python
import functools

import jax
import jax.numpy as jnp
from jax import lax
from jax.experimental import pallas as pl
from jax.experimental.pallas import tpu as pltpu
from jax.sharding import PartitionSpec as P

MESH = pl.DeviceIdType.MESH
T = 128
ROWS = 16
SLOTS = 20
ITERS = 2
PARTS = (48, 40, 40)
STARTS = (0, 48, 88)
ORDERS = (("z", "x", "y"), ("y", "z", "x"), ("x", "y", "z"))
STEPS = (1, 3, 2)
FAR_STEP = 16
STAGED = 6
HIGH = lax.Precision.HIGHEST
F32 = jnp.float32


def split(a):
    hi = a.astype(jnp.bfloat16)
    return hi, (a - hi.astype(F32)).astype(jnp.bfloat16)


def inverse_factor(m_ref, v_ref):
    lane = lax.broadcasted_iota(jnp.int32, (8, T), 1)
    sub = lax.broadcasted_iota(jnp.int32, (8, T), 0)
    v_ref[...] = (
        lax.broadcasted_iota(jnp.int32, (T, T), 0) == lax.broadcasted_iota(jnp.int32, (T, T), 1)
    ).astype(F32)

    def block(b, carry):
        base = pl.multiple_of(b * 8, 8)
        p = m_ref[pl.ds(base, 8), :]
        q = v_ref[pl.ds(base, 8), :]
        cols = [
            jnp.broadcast_to(jnp.sum(jnp.where(lane == base + j, p, 0.0), axis=1, keepdims=True), (8, T))
            for j in range(8)
        ]
        for j in range(8):
            pivot = jnp.broadcast_to(cols[j][j : j + 1, :], (8, T))
            scale = lax.rsqrt(pivot)
            scale = scale * (1.5 - 0.5 * pivot * scale * scale)
            coef = jnp.where(sub > j, cols[j] * scale, 0.0)
            for m in range(j + 1, 8):
                cols[m] = cols[m] - coef * (jnp.broadcast_to(cols[m][j : j + 1, :], (8, T)) * scale)
            prow = jnp.broadcast_to(p[j : j + 1, :], (8, T)) * scale
            qrow = jnp.broadcast_to(q[j : j + 1, :], (8, T)) * scale
            p = jnp.where(sub == j, prow, p - coef * prow)
            q = jnp.where(sub == j, qrow, q - coef * qrow)
        v_ref[pl.ds(base, 8), :] = q
        below = jnp.where(lane >= base + 8, p, 0.0)
        both = jnp.concatenate([p, q], axis=1)
        update = lax.dot_general(
            below, both, (((0,), (0,)), ((), ())), precision=HIGH, preferred_element_type=F32
        )
        m_ref[...] -= update[:, :T]
        v_ref[...] -= update[:, T:]
        return carry

    lax.fori_loop(0, T // 8, block, 0)


def index_tables(cols_ref, counts_ref, x, y, z, c):
    sub = lax.broadcasted_iota(jnp.int32, (ROWS, T), 0)
    lane = lax.broadcasted_iota(jnp.int32, (ROWS, T), 1)
    counts = jnp.zeros((ROWS, T), jnp.int32)
    for r in range(ROWS):
        counts = jnp.where(sub == r, counts_ref[r], counts)
    own = jnp.full((ROWS, T), ROWS, jnp.int32)
    slots = []
    total = jnp.zeros((ROWS, T), jnp.int32)
    for s in range(SLOTS):
        col = jnp.broadcast_to(cols_ref[:, s : s + 1], (ROWS, T))
        owner, local = col >> 4, col & 15
        away = {"x": (x - owner) & 3, "y": (y - (owner >> 3)) & 3, "z": (z - (owner >> 5)) & 3}
        dc = (c - (owner >> 2)) & 1
        place = away["x"] * 32 + away["y"] * 8 + away["z"] * 2 + dc
        far = place != 0
        own = jnp.where((lane == s) & ~far & (s < counts), local, own)
        slots.append((far, local, place, [(away[a3] * 2 + dc) * 16 + away[a2] * 4 + away[a1] for a1, a2, a3 in ORDERS], total))
        total = total + jnp.where(far, 1, 0)
    before = jnp.zeros((ROWS, T), jnp.int32)
    for r in range(ROWS - 1):
        before = before + jnp.where(sub > r, jnp.broadcast_to(total[r : r + 1, :], (ROWS, T)), 0)
    rows = [jnp.zeros((ROWS, T), jnp.int32) for _ in range(6)]
    for s, (far, local, place, places, rank) in enumerate(slots):
        hot = far & (lane == before + rank)
        rows[0] = rows[0] + jnp.where(far & (lane == place), local, 0)
        for n, value in enumerate([sub * SLOTS + s, *places, jnp.where(rank > 0, 1, 0)]):
            rows[n + 1] = rows[n + 1] + jnp.where(hot, value, 0)
    last = jnp.where(total > 0, jnp.minimum(before + total - 1, 127), 127)
    rows.append(jnp.where(lane == sub, last, 0))
    lists = [jnp.sum(row, axis=0, keepdims=True) for row in rows]
    return own, lists


def kernel(
    tiles_hbm, block_ref, cols_ref, counts_ref, out_ref,
    whi, wlo, work, ag1, ag2, ag3, ag4, ag5, ag6, ag7, ag8, ag9,
    st0, st1, st2, xr0, xr1, xr2, fn0, fn1, fn2, xs, xcat, inv, icol, ic0, ic1, ic2,
    gsrc, gpart, gline, gout, factor, wtab, stab, own_vec, list_vec, own_ref, list_ref,
    load_sem, s1s, s1r, fs, fr, is_, ir, s2s, s2r, s3s, s3r, loc_sem, ws, wr, tab_sem, own_sem, list_sem, gs, gr, free_in, free_out,
):
    ag = ((None, ag1, ag2, ag3), (None, ag4, ag5, ag6), (None, ag7, ag8, ag9))
    st, xr, fn, ic = (st0, st1, st2), (xr0, xr1, xr2), (fn0, fn1, fn2), (ic0, ic1, ic2)
    acc = out_ref
    row, grp = lax.axis_index("row"), lax.axis_index("grp")
    at = {"z": row // 8, "y": (row // 2) % 4, "x": grp, "c": row % 2}

    def device(**by):
        v = {k: lax.rem(at[k] + by[k], 2 if k == "c" else 4) if k in by else at[k] for k in at}
        return (v["z"] * 8 + v["y"] * 2 + v["c"], v["x"])

    def load_copy(r):
        place = pl.multiple_of(lax.rem(r, STAGED) * SLOTS, SLOTS)
        return pltpu.make_async_copy(tiles_hbm.at[r], work.at[pl.ds(place, SLOTS)], load_sem.at[r])

    for r in range(STAGED):
        load_copy(r).start()

    barrier = pltpu.get_barrier_semaphore()
    same_core = [{a: d} for a in "xyz" for d in STEPS]
    all_peers = same_core + [{a: d, "c": 1} for a in "xyz" for d in STEPS] + [{"c": 1}]
    for by in all_peers:
        pl.semaphore_signal(barrier, inc=1, device_id=device(**by), device_id_type=MESH)
    own, lists = index_tables(cols_ref, counts_ref, at["x"], at["y"], at["z"], at["c"])
    own_vec[...] = own
    for n, row_list in enumerate(lists):
        list_vec[n] = row_list
    own_table = pltpu.make_async_copy(own_vec, own_ref, own_sem)
    own_table.start()
    list_table = pltpu.make_async_copy(list_vec, list_ref, list_sem)
    list_table.start()
    pl.semaphore_wait(barrier, len(all_peers))

    def gather_copy(i, d, it):
        source = xs if it else block_ref
        return pltpu.make_async_remote_copy(
            source.at[:, pl.ds(STARTS[i], PARTS[i])], ag[i][d], s1s.at[i, d], s1r.at[i, d],
            device_id=device(**{ORDERS[i][0]: d}), device_id_type=MESH,
        )

    half = ROWS // 2

    def forward_copy(i, d):
        part = pl.ds(0 if d == 1 else half, half)
        return pltpu.make_async_remote_copy(
            ag[i][d].at[part], ag[i][2].at[part], fs.at[i, d], fr.at[i, d],
            device_id=device(**{ORDERS[i][0]: d}), device_id_type=MESH,
        )

    def root_copy(i, d):
        return pltpu.make_async_remote_copy(
            icol.at[pl.ds(STARTS[i], PARTS[i])], ic[i].at[d], is_.at[i, d], ir.at[i, d],
            device_id=device(**{ORDERS[i][0]: d}), device_id_type=MESH,
        )

    wtab[0, 0, 0, 0] = lists[0]

    def table_copies(stage):
        axis = "zyxc"[stage]
        copies = []
        for d in (1,) if axis == "c" else STEPS:
            src, dst = {
                "z": (wtab.at[0, 0, 0, 0], wtab.at[0, 0, 0, d]),
                "y": (wtab.at[0, 0, 0], wtab.at[0, 0, d]),
                "x": (wtab.at[0, 0], wtab.at[0, d]),
                "c": (wtab.at[0], wtab.at[d]),
            }[axis]
            copies.append(
                pltpu.make_async_remote_copy(
                    src, dst, ws.at[stage, d], wr.at[stage, d], device_id=device(**{axis: d}), device_id_type=MESH
                )
            )
        return copies

    lane = lax.broadcasted_iota(jnp.int32, (T, T), 1)

    def take_row(r, columns):
        load_copy(r).wait()
        place = lax.rem(r, STAGED) * SLOTS
        count = counts_ref[r]

        def add(s, total):
            tile = work[place + s]
            hi, lo = split(tile)
            whi[r, s] = hi
            wlo[r, s] = lo
            return total + tile * jnp.where(s < count, 1.0, 0.0)

        total = lax.fori_loop(0, SLOTS, add, jnp.zeros((T, T), F32), unroll=4)
        root = 1.0 / jnp.sqrt(jnp.sum(total, axis=1, keepdims=True))
        inv[r] = jnp.broadcast_to(root, (T, T))
        return jnp.where(lane == r, root, columns)

    def take_and_load(r, columns):
        columns = take_row(r, columns)
        load_copy(r + STAGED).start()
        return columns

    columns = jnp.zeros((T, T), F32)
    for stage in range(4):
        copies = table_copies(stage)
        for copy in copies:
            copy.start()
        if stage == 0:
            for d in (1, 3):
                for i in range(3):
                    gather_copy(i, d, 0).start()
        low, high = stage * 4, stage * 4 + 4
        middle = min(max(ROWS - STAGED, low), high)
        columns = lax.fori_loop(low, middle, take_and_load, columns)
        columns = lax.fori_loop(middle, high, take_row, columns)
        for copy in copies:
            copy.wait()
    icol[...] = columns
    for d in STEPS:
        for i in range(3):
            root_copy(i, d).start()
    table = pltpu.make_async_copy(wtab, stab, tab_sem)
    table.start()

    xcat[ROWS] = jnp.zeros((T, 2 * T), jnp.bfloat16)
    for i in range(3):
        fn[i][0, 0] = jnp.zeros((PARTS[i], T), F32)

    def put(r, value):
        xs[r] = value
        xcat[r] = jnp.concatenate(split(value), axis=1)

    def begin(r, carry):
        put(r, block_ref[r] * inv[r])
        return carry

    lax.fori_loop(0, ROWS, begin, 0)
    table.wait()
    own_table.wait()
    list_table.wait()

    def second_copy(i, d2, d1):
        return pltpu.make_async_remote_copy(
            st[i].at[d2 - 1, d1], xr[i].at[d2, d1], s2s.at[i, d2, d1], s2r.at[i, d2, d1],
            device_id=device(**{ORDERS[i][1]: d2}), device_id_type=MESH,
        )

    def select(i, d1, it):
        a1, a2, a3 = ORDERS[i]
        for d2 in range(4):

            def pick(e, carry):
                d3, dc = e // 2, e % 2
                off = {a1: d1, a2: d2, a3: d3}
                back = {a1: 0, a2: (4 - d2) % 4, a3: lax.rem(4 - d3, 4)}
                place = ((off["x"] * 4 + off["y"]) * 4 + off["z"]) * 2 + dc
                which = stab[dc, back["x"], back["y"], back["z"], 0, place]
                if d1 == 0:
                    value = xs[which, STARTS[i] : STARTS[i] + PARTS[i]]
                else:
                    value = ag[i][d1][which]
                if d1 and it == 0:
                    roots = jnp.where(lane[: PARTS[i]] == which, ic[i][d1], 0.0)
                    value = value * jnp.sum(roots, axis=1, keepdims=True)
                if d2 == 0:
                    xr[i][0, d1, e] = value
                else:
                    st[i][d2 - 1, d1, e] = value
                return carry

            lax.fori_loop(0, 8, pick, 0, unroll=4)

    def third_start(i, d2):
        a3 = ORDERS[i][2]
        for e in (2, 6, 3, 7, 4, 5, 1):
            by = {a3: e // 2} if e >= 2 else {}
            if e % 2:
                by["c"] = 1
            pltpu.make_async_remote_copy(
                xr[i].at[d2, :, e], fn[i].at[e, pl.ds(d2 * 4, 4)], s3s.at[i], s3r.at[i],
                device_id=device(**by), device_id_type=MESH,
            ).start()

    def third_all(i):
        return pltpu.make_async_remote_copy(
            fn[i].at[pl.ds(1, 7)], fn[i].at[pl.ds(1, 7)], s3s.at[i], s3r.at[i],
            device_id=device(c=1), device_id_type=MESH,
        )

    def own_copy(i, d2):
        first = 1 if d2 == 0 else 0
        return pltpu.make_async_copy(
            xr[i].at[d2, pl.ds(first, 4 - first), 0],
            fn[i].at[0, pl.ds(d2 * 4 + first, 4 - first)],
            loc_sem.at[i, d2],
        )

    dot = functools.partial(jnp.dot, preferred_element_type=F32)

    def home(r, carry):
        total = jnp.zeros((T, 2 * T), F32)
        small = jnp.zeros((T, T), F32)
        for s in range(0, SLOTS, 2):
            b = jnp.concatenate([xcat[own_ref[r, s]], xcat[own_ref[r, s + 1]]], axis=0)
            total = total + dot(jnp.concatenate([whi[r, s], whi[r, s + 1]], axis=1), b)
            small = small + dot(jnp.concatenate([wlo[r, s], wlo[r, s + 1]], axis=1), b[:, :T])
        acc[r] = total[:, :T] + (total[:, T:] + small)
        return carry

    def far_products(group, running):
        values = []
        for k in range(FAR_STEP):
            k = group * FAR_STEP + k
            slot = list_ref[1, 0, k]
            pieces = []
            for i in range(3):
                where = list_ref[2 + i, 0, k]
                pieces.append(fn[i][where // 16, lax.rem(where, 16)])
            hi, lo = split(jnp.concatenate(pieces, axis=0))
            r, s = slot // SLOTS, lax.rem(slot, SLOTS)
            wide = dot(whi[r, s], jnp.concatenate([hi, lo], axis=1))
            values.append(wide[:, :T] + (wide[:, T:] + dot(wlo[r, s], hi)))
        for k in range(FAR_STEP):
            running = jnp.where(list_ref[5, 0, group * FAR_STEP + k] > 0, running, 0.0) + values[k]
            work[group * FAR_STEP + k] = running
        return running

    def add_far(r):
        return (acc[r] + work[list_ref[6, 0, r]]) * inv[r]

    group = [(dx, dc) for dx in range(4) for dc in range(2) if dx or dc]
    mine = pl.multiple_of((at["x"] * 2 + at["c"]) * 16, 16)

    def gram_copies(it, stage):
        copies = []
        if stage in (1, 2):
            axis = "yz"[stage - 1]
            for d in STEPS:
                copies.append(
                    pltpu.make_async_remote_copy(
                        gline.at[it, stage - 1, 0], gline.at[it, stage - 1, d],
                        gs.at[it, stage, d], gr.at[it, stage, d],
                        device_id=device(**{axis: d}), device_id_type=MESH,
                    )
                )
            return copies
        for dx, dc in group:
            by = {k: v for k, v in (("x", dx), ("c", dc)) if v}
            e = dx * 2 + dc
            if stage == 0:
                theirs = lax.rem(at["x"] + dx, 4) * 2 + lax.rem(at["c"] + dc, 2)
                src, dst = gsrc.at[it, pl.ds(pl.multiple_of(theirs * 16, 16), 16)], gpart.at[it, e]
            else:
                src = dst = gout.at[it, pl.ds(mine, 16)]
            copies.append(
                pltpu.make_async_remote_copy(
                    src, dst, gs.at[it, stage, e], gr.at[it, stage, e], device_id=device(**by), device_id_type=MESH
                )
            )
        return copies

    def gram_start(it, stage):
        for copy in gram_copies(it, stage):
            copy.start()

    def gram_finish(it, stage):
        for copy in gram_copies(it, stage):
            copy.wait()
        if stage == 0:
            total = gsrc[it, pl.ds(mine, 16)]
            for dx, dc in group:
                total = total + gpart[it, dx * 2 + dc]
        elif stage < 3:
            total = (gline[it, stage - 1, 0] + gline[it, stage - 1, 1]) + (gline[it, stage - 1, 2] + gline[it, stage - 1, 3])
        if stage < 2:
            gline[it, stage, 0] = total
        elif stage == 2:
            gout[it, pl.ds(mine, 16)] = total

    def local_gram(it):
        def add(r, total):
            a = acc[r]
            return total + lax.dot_general(
                a, a, (((0,), (0,)), ((), ())), precision=HIGH, preferred_element_type=F32
            )

        gsrc[it] = lax.fori_loop(0, ROWS, add, jnp.zeros((T, T), F32), unroll=4)

    root_total = jnp.sqrt(F32(ROWS * T * 128))

    def normalised(value):
        return root_total * lax.dot_general(
            value, factor[...], (((1,), (1,)), ((), ())), precision=HIGH, preferred_element_type=F32
        )

    for it in range(ITERS):

        def forward_start():
            for d in (1, 3):
                for i in range(3):
                    gather_copy(i, d, it).wait_recv()
                    forward_copy(i, d).start()

        def second_start(d1s, d2s):
            for pair in d2s:
                for d1 in d1s:
                    for i in range(3):
                        for d2 in pair:
                            second_copy(i, d2, d1).start()

        if it:
            pl.semaphore_wait(free_in, len(same_core))
            for d in (1, 3):
                for i in range(3):
                    gather_copy(i, d, it).start()
        else:
            forward_start()
        for i in range(3):
            select(i, 0, it)
        second_start((0,), ((2,), (1, 3)))
        if it:
            local_gram(0)
            gram_start(0, 0)
            lax.fori_loop(0, 5, home, 0)
            gram_finish(0, 0)
            gram_start(0, 1)
            forward_start()
        else:
            for d in STEPS:
                for i in range(3):
                    root_copy(i, d).wait_recv()
        for d in (1, 3):
            for i in range(3):
                select(i, d, it)
        second_start((1, 3), ((2,), (1, 3)))
        if it:
            gram_finish(0, 1)
            gram_start(0, 2)
            lax.fori_loop(5, 9, home, 0)
        for i in range(3):
            for d in (1, 3):
                forward_copy(i, d).wait_recv()
            select(i, 2, it)
        second_start((2,), ((2,), (1, 3)))
        if it:
            pl.semaphore_wait(free_out, len(all_peers))
        for i in range(3):
            third_start(i, 0)
            own_copy(i, 0).start()
        if it:
            gram_finish(0, 2)
            gram_start(0, 3)
        lax.fori_loop(9 if it else 0, ROWS, home, 0)
        for d2 in (2, 1, 3):
            for i in (1, 2, 0):
                for d1 in range(4):
                    second_copy(i, d2, d1).wait_recv()
                third_start(i, d2)
                own_copy(i, d2).start()
        if it:
            gram_finish(0, 3)
            inverse_factor(gout.at[0], factor)
        for i in range(3):
            for d in (1, 3):
                gather_copy(i, d, it).wait_send()
                forward_copy(i, d).wait_send()
            for d in STEPS:
                if it == 0:
                    root_copy(i, d).wait_send()
                for d1 in range(4):
                    second_copy(i, d, d1).wait_send()
            third_all(i).wait_send()
            for d2 in range(4):
                own_copy(i, d2).wait()
        if it == 0:
            for by in same_core:
                pl.semaphore_signal(free_in, inc=1, device_id=device(**by), device_id_type=MESH)
        for i in range(3):
            third_all(i).wait_recv()
        lax.fori_loop(0, 128 // FAR_STEP, far_products, jnp.zeros((T, T), F32))

        if it == 0:
            for by in all_peers:
                pl.semaphore_signal(free_out, inc=1, device_id=device(**by), device_id_type=MESH)

            def close(r, carry):
                image = add_far(r)
                acc[r] = image
                put(r, image * inv[r])
                return carry

            lax.fori_loop(0, ROWS, close, 0, unroll=2)
        else:

            def close_last(r, carry):
                acc[r] = normalised(add_far(r))
                return carry

            lax.fori_loop(0, ROWS, close_last, 0, unroll=4)
    local_gram(1)
    for stage in range(4):
        gram_start(1, stage)
        gram_finish(1, stage)
    inverse_factor(gout.at[1], factor)

    def finish(r, carry):
        out_ref[r] = normalised(acc[r])
        return carry

    lax.fori_loop(0, ROWS, finish, 0, unroll=4)


def per_device(tiles, tile_cols, tile_counts, block):
    smem, vmem = pl.BlockSpec(memory_space=pltpu.SMEM), pl.BlockSpec(memory_space=pltpu.VMEM)
    dma = pltpu.SemaphoreType.DMA
    out = pl.pallas_call(
        kernel,
        out_shape=jax.ShapeDtypeStruct((ROWS, T, T), F32),
        in_specs=[pl.BlockSpec(memory_space=pl.ANY), vmem, vmem, smem],
        out_specs=vmem,
        scratch_shapes=[
            pltpu.VMEM((ROWS, SLOTS, T, T), jnp.bfloat16),
            pltpu.VMEM((ROWS, SLOTS, T, T), jnp.bfloat16),
            pltpu.VMEM((128, T, T), F32),
            *[pltpu.VMEM((ROWS, n, T), F32) for n in PARTS for _ in range(3)],
            *[pltpu.VMEM((3, 4, 8, n, T), F32) for n in PARTS],
            *[pltpu.VMEM((4, 4, 8, n, T), F32) for n in PARTS],
            *[pltpu.VMEM((8, 16, n, T), F32) for n in PARTS],
            pltpu.VMEM((ROWS, T, T), F32),
            pltpu.VMEM((ROWS + 1, T, 2 * T), jnp.bfloat16),
            pltpu.VMEM((ROWS, T, T), F32),
            pltpu.VMEM((T, T), F32),
            *[pltpu.VMEM((4, n, T), F32) for n in PARTS],
            pltpu.VMEM((2, T, T), F32),
            pltpu.VMEM((2, 8, 16, T), F32),
            pltpu.VMEM((2, 2, 4, 16, T), F32),
            pltpu.VMEM((2, T, T), F32),
            pltpu.VMEM((T, T), F32),
            pltpu.VMEM((2, 4, 4, 4, 1, T), jnp.int32),
            pltpu.SMEM((2, 4, 4, 4, 1, T), jnp.int32),
            pltpu.VMEM((ROWS, T), jnp.int32),
            pltpu.VMEM((7, 1, T), jnp.int32),
            pltpu.SMEM((ROWS, T), jnp.int32),
            pltpu.SMEM((7, 1, T), jnp.int32),
            dma((ROWS,)),
            *[dma((3, 4)) for _ in range(6)],
            dma((3, 4, 4)),
            dma((3, 4, 4)),
            dma((3,)),
            dma((3,)),
            dma((3, 4)),
            dma((4, 4)),
            dma((4, 4)),
            dma,
            dma,
            dma,
            dma((2, 4, 8)),
            dma((2, 4, 8)),
            pltpu.SemaphoreType.REGULAR,
            pltpu.SemaphoreType.REGULAR,
        ],
        compiler_params=pltpu.CompilerParams(
            collective_id=0, has_side_effects=True, vmem_limit_bytes=63 * 2**20
        ),
    )(tiles, block.reshape(ROWS, T, T), tile_cols, tile_counts)
    return out.reshape(ROWS * T, T)


def solution(mesh):
    shard = ("row", "grp")
    return jax.shard_map(
        per_device,
        mesh=mesh,
        in_specs=(P(shard, None, None, None), P(shard, None), P(shard), P(shard, None)),
        out_specs=P(shard, None),
        check_vma=False,
    )
```

```python
import functools

import jax
import jax.numpy as jnp
from jax import lax
from jax.experimental import pallas as pl
from jax.experimental.pallas import tpu as pltpu
from jax.sharding import PartitionSpec as P

MESH = pl.DeviceIdType.MESH
T = 128
ROWS = 16
SLOTS = 20
ITERS = 2
PARTS = (48, 40, 40)
STARTS = (0, 48, 88)
ORDERS = (("z", "x", "y"), ("y", "z", "x"), ("x", "y", "z"))
STEPS = (1, 3, 2)
FAR_STEP = 16
STAGED = 6
HIGH = lax.Precision.HIGHEST
F32 = jnp.float32


def split(a):
    hi = a.astype(jnp.bfloat16)
    return hi, (a - hi.astype(F32)).astype(jnp.bfloat16)


def inverse_factor(m_ref, v_ref):
    lane = lax.broadcasted_iota(jnp.int32, (8, T), 1)
    sub = lax.broadcasted_iota(jnp.int32, (8, T), 0)
    v_ref[...] = (
        lax.broadcasted_iota(jnp.int32, (T, T), 0) == lax.broadcasted_iota(jnp.int32, (T, T), 1)
    ).astype(F32)

    def block(b, carry):
        base = pl.multiple_of(b * 8, 8)
        p = m_ref[pl.ds(base, 8), :]
        q = v_ref[pl.ds(base, 8), :]
        cols = [
            jnp.broadcast_to(jnp.sum(jnp.where(lane == base + j, p, 0.0), axis=1, keepdims=True), (8, T))
            for j in range(8)
        ]
        for j in range(8):
            pivot = jnp.broadcast_to(cols[j][j : j + 1, :], (8, T))
            scale = lax.rsqrt(pivot)
            scale = scale * (1.5 - 0.5 * pivot * scale * scale)
            coef = jnp.where(sub > j, cols[j] * scale, 0.0)
            for m in range(j + 1, 8):
                cols[m] = cols[m] - coef * (jnp.broadcast_to(cols[m][j : j + 1, :], (8, T)) * scale)
            prow = jnp.broadcast_to(p[j : j + 1, :], (8, T)) * scale
            qrow = jnp.broadcast_to(q[j : j + 1, :], (8, T)) * scale
            p = jnp.where(sub == j, prow, p - coef * prow)
            q = jnp.where(sub == j, qrow, q - coef * qrow)
        v_ref[pl.ds(base, 8), :] = q
        below = jnp.where(lane >= base + 8, p, 0.0)
        both = jnp.concatenate([p, q], axis=1)
        update = lax.dot_general(
            below, both, (((0,), (0,)), ((), ())), precision=HIGH, preferred_element_type=F32
        )
        m_ref[...] -= update[:, :T]
        v_ref[...] -= update[:, T:]
        return carry

    lax.fori_loop(0, T // 8, block, 0)


def index_tables(cols_ref, counts_ref, x, y, z, c):
    sub = lax.broadcasted_iota(jnp.int32, (ROWS, T), 0)
    lane = lax.broadcasted_iota(jnp.int32, (ROWS, T), 1)
    counts = jnp.zeros((ROWS, T), jnp.int32)
    for r in range(ROWS):
        counts = jnp.where(sub == r, counts_ref[r], counts)
    own = jnp.full((ROWS, T), ROWS, jnp.int32)
    slots = []
    total = jnp.zeros((ROWS, T), jnp.int32)
    for s in range(SLOTS):
        col = jnp.broadcast_to(cols_ref[:, s : s + 1], (ROWS, T))
        owner, local = col >> 4, col & 15
        away = {"x": (x - owner) & 3, "y": (y - (owner >> 3)) & 3, "z": (z - (owner >> 5)) & 3}
        dc = (c - (owner >> 2)) & 1
        place = away["x"] * 32 + away["y"] * 8 + away["z"] * 2 + dc
        far = place != 0
        own = jnp.where((lane == s) & ~far & (s < counts), local, own)
        slots.append((far, local, place, [(away[a3] * 2 + dc) * 16 + away[a2] * 4 + away[a1] for a1, a2, a3 in ORDERS], total))
        total = total + jnp.where(far, 1, 0)
    before = jnp.zeros((ROWS, T), jnp.int32)
    for r in range(ROWS - 1):
        before = before + jnp.where(sub > r, jnp.broadcast_to(total[r : r + 1, :], (ROWS, T)), 0)
    rows = [jnp.zeros((ROWS, T), jnp.int32) for _ in range(6)]
    for s, (far, local, place, places, rank) in enumerate(slots):
        hot = far & (lane == before + rank)
        rows[0] = rows[0] + jnp.where(far & (lane == place), local, 0)
        for n, value in enumerate([sub * SLOTS + s, *places, jnp.where(rank > 0, 1, 0)]):
            rows[n + 1] = rows[n + 1] + jnp.where(hot, value, 0)
    last = jnp.where(total > 0, jnp.minimum(before + total - 1, 127), 127)
    rows.append(jnp.where(lane == sub, last, 0))
    lists = [jnp.sum(row, axis=0, keepdims=True) for row in rows]
    return own, lists


def kernel(
    tiles_hbm, block_ref, cols_ref, counts_ref, out_ref,
    whi, wlo, work, ag1, ag2, ag3, ag4, ag5, ag6, ag7, ag8, ag9,
    st0, st1, st2, xr0, xr1, xr2, fn0, fn1, fn2, xs, xcat, inv, icol, ic0, ic1, ic2,
    gsrc, gpart, gline, gout, factor, wtab, stab, own_vec, list_vec, own_ref, list_ref,
    load_sem, s1s, s1r, fs, fr, is_, ir, s2s, s2r, s3s, s3r, loc_sem, ws, wr, tab_sem, own_sem, list_sem, gs, gr, free_in, free_out,
):
    ag = ((None, ag1, ag2, ag3), (None, ag4, ag5, ag6), (None, ag7, ag8, ag9))
    st, xr, fn, ic = (st0, st1, st2), (xr0, xr1, xr2), (fn0, fn1, fn2), (ic0, ic1, ic2)
    acc = out_ref
    row, grp = lax.axis_index("row"), lax.axis_index("grp")
    at = {"z": row // 8, "y": (row // 2) % 4, "x": grp, "c": row % 2}

    def device(**by):
        v = {k: lax.rem(at[k] + by[k], 2 if k == "c" else 4) if k in by else at[k] for k in at}
        return (v["z"] * 8 + v["y"] * 2 + v["c"], v["x"])

    def load_copy(r):
        place = pl.multiple_of(lax.rem(r, STAGED) * SLOTS, SLOTS)
        return pltpu.make_async_copy(tiles_hbm.at[r], work.at[pl.ds(place, SLOTS)], load_sem.at[r])

    for r in range(STAGED):
        load_copy(r).start()

    barrier = pltpu.get_barrier_semaphore()
    same_core = [{a: d} for a in "xyz" for d in STEPS]
    all_peers = same_core + [{a: d, "c": 1} for a in "xyz" for d in STEPS] + [{"c": 1}]
    for by in all_peers:
        pl.semaphore_signal(barrier, inc=1, device_id=device(**by), device_id_type=MESH)
    own, lists = index_tables(cols_ref, counts_ref, at["x"], at["y"], at["z"], at["c"])
    own_vec[...] = own
    for n, row_list in enumerate(lists):
        list_vec[n] = row_list
    own_table = pltpu.make_async_copy(own_vec, own_ref, own_sem)
    own_table.start()
    list_table = pltpu.make_async_copy(list_vec, list_ref, list_sem)
    list_table.start()
    pl.semaphore_wait(barrier, len(all_peers))

    def gather_copy(i, d, it):
        source = xs if it else block_ref
        return pltpu.make_async_remote_copy(
            source.at[:, pl.ds(STARTS[i], PARTS[i])], ag[i][d], s1s.at[i, d], s1r.at[i, d],
            device_id=device(**{ORDERS[i][0]: d}), device_id_type=MESH,
        )

    half = ROWS // 2

    def forward_copy(i, d):
        part = pl.ds(0 if d == 1 else half, half)
        return pltpu.make_async_remote_copy(
            ag[i][d].at[part], ag[i][2].at[part], fs.at[i, d], fr.at[i, d],
            device_id=device(**{ORDERS[i][0]: d}), device_id_type=MESH,
        )

    def root_copy(i, d):
        return pltpu.make_async_remote_copy(
            icol.at[pl.ds(STARTS[i], PARTS[i])], ic[i].at[d], is_.at[i, d], ir.at[i, d],
            device_id=device(**{ORDERS[i][0]: d}), device_id_type=MESH,
        )

    wtab[0, 0, 0, 0] = lists[0]

    def table_copies(stage):
        axis = "zyxc"[stage]
        copies = []
        for d in (1,) if axis == "c" else STEPS:
            src, dst = {
                "z": (wtab.at[0, 0, 0, 0], wtab.at[0, 0, 0, d]),
                "y": (wtab.at[0, 0, 0], wtab.at[0, 0, d]),
                "x": (wtab.at[0, 0], wtab.at[0, d]),
                "c": (wtab.at[0], wtab.at[d]),
            }[axis]
            copies.append(
                pltpu.make_async_remote_copy(
                    src, dst, ws.at[stage, d], wr.at[stage, d], device_id=device(**{axis: d}), device_id_type=MESH
                )
            )
        return copies

    lane = lax.broadcasted_iota(jnp.int32, (T, T), 1)

    def take_row(r, columns):
        load_copy(r).wait()
        place = lax.rem(r, STAGED) * SLOTS
        count = counts_ref[r]

        def add(s, total):
            tile = work[place + s]
            hi, lo = split(tile)
            whi[r, s] = hi
            wlo[r, s] = lo
            return total + tile * jnp.where(s < count, 1.0, 0.0)

        total = lax.fori_loop(0, SLOTS, add, jnp.zeros((T, T), F32), unroll=8)
        root = 1.0 / jnp.sqrt(jnp.sum(total, axis=1, keepdims=True))
        inv[r] = jnp.broadcast_to(root, (T, T))
        return jnp.where(lane == r, root, columns)

    def take_and_load(r, columns):
        columns = take_row(r, columns)
        load_copy(r + STAGED).start()
        return columns

    columns = jnp.zeros((T, T), F32)
    for stage in range(4):
        copies = table_copies(stage)
        for copy in copies:
            copy.start()
        if stage == 0:
            for d in (1, 3):
                for i in range(3):
                    gather_copy(i, d, 0).start()
        low, high = stage * 4, stage * 4 + 4
        middle = min(max(ROWS - STAGED, low), high)
        columns = lax.fori_loop(low, middle, take_and_load, columns)
        columns = lax.fori_loop(middle, high, take_row, columns)
        for copy in copies:
            copy.wait()
    icol[...] = columns
    for d in STEPS:
        for i in range(3):
            root_copy(i, d).start()
    table = pltpu.make_async_copy(wtab, stab, tab_sem)
    table.start()

    xcat[ROWS] = jnp.zeros((T, 2 * T), jnp.bfloat16)
    for i in range(3):
        fn[i][0, 0] = jnp.zeros((PARTS[i], T), F32)

    def put(r, value):
        xs[r] = value
        xcat[r] = jnp.concatenate(split(value), axis=1)

    def begin(r, carry):
        put(r, block_ref[r] * inv[r])
        return carry

    lax.fori_loop(0, ROWS, begin, 0)
    table.wait()
    own_table.wait()
    list_table.wait()

    def second_copy(i, d2, d1):
        return pltpu.make_async_remote_copy(
            st[i].at[d2 - 1, d1], xr[i].at[d2, d1], s2s.at[i, d2, d1], s2r.at[i, d2, d1],
            device_id=device(**{ORDERS[i][1]: d2}), device_id_type=MESH,
        )

    def select(i, d1, it):
        a1, a2, a3 = ORDERS[i]
        for d2 in range(4):

            def pick(e, carry):
                d3, dc = e // 2, e % 2
                off = {a1: d1, a2: d2, a3: d3}
                back = {a1: 0, a2: (4 - d2) % 4, a3: lax.rem(4 - d3, 4)}
                place = ((off["x"] * 4 + off["y"]) * 4 + off["z"]) * 2 + dc
                which = stab[dc, back["x"], back["y"], back["z"], 0, place]
                if d1 == 0:
                    value = xs[which, STARTS[i] : STARTS[i] + PARTS[i]]
                else:
                    value = ag[i][d1][which]
                if d1 and it == 0:
                    roots = jnp.where(lane[: PARTS[i]] == which, ic[i][d1], 0.0)
                    value = value * jnp.sum(roots, axis=1, keepdims=True)
                if d2 == 0:
                    xr[i][0, d1, e] = value
                else:
                    st[i][d2 - 1, d1, e] = value
                return carry

            lax.fori_loop(0, 8, pick, 0, unroll=8)

    def third_start(i, d2):
        a3 = ORDERS[i][2]
        for e in (2, 6, 3, 7, 4, 5, 1):
            by = {a3: e // 2} if e >= 2 else {}
            if e % 2:
                by["c"] = 1
            pltpu.make_async_remote_copy(
                xr[i].at[d2, :, e], fn[i].at[e, pl.ds(d2 * 4, 4)], s3s.at[i], s3r.at[i],
                device_id=device(**by), device_id_type=MESH,
            ).start()

    def third_all(i):
        return pltpu.make_async_remote_copy(
            fn[i].at[pl.ds(1, 7)], fn[i].at[pl.ds(1, 7)], s3s.at[i], s3r.at[i],
            device_id=device(c=1), device_id_type=MESH,
        )

    def own_copy(i, d2):
        first = 1 if d2 == 0 else 0
        return pltpu.make_async_copy(
            xr[i].at[d2, pl.ds(first, 4 - first), 0],
            fn[i].at[0, pl.ds(d2 * 4 + first, 4 - first)],
            loc_sem.at[i, d2],
        )

    dot = functools.partial(jnp.dot, preferred_element_type=F32)

    def home(r, carry):
        total = jnp.zeros((T, 2 * T), F32)
        small = jnp.zeros((T, T), F32)
        for s in range(0, SLOTS, 2):
            b = jnp.concatenate([xcat[own_ref[r, s]], xcat[own_ref[r, s + 1]]], axis=0)
            total = total + dot(jnp.concatenate([whi[r, s], whi[r, s + 1]], axis=1), b)
            small = small + dot(jnp.concatenate([wlo[r, s], wlo[r, s + 1]], axis=1), b[:, :T])
        acc[r] = total[:, :T] + (total[:, T:] + small)
        return carry

    def far_products(group, running):
        values = []
        for k in range(FAR_STEP):
            k = group * FAR_STEP + k
            slot = list_ref[1, 0, k]
            pieces = []
            for i in range(3):
                where = list_ref[2 + i, 0, k]
                pieces.append(fn[i][where // 16, lax.rem(where, 16)])
            hi, lo = split(jnp.concatenate(pieces, axis=0))
            r, s = slot // SLOTS, lax.rem(slot, SLOTS)
            wide = dot(whi[r, s], jnp.concatenate([hi, lo], axis=1))
            values.append(wide[:, :T] + (wide[:, T:] + dot(wlo[r, s], hi)))
        for k in range(FAR_STEP):
            running = jnp.where(list_ref[5, 0, group * FAR_STEP + k] > 0, running, 0.0) + values[k]
            work[group * FAR_STEP + k] = running
        return running

    def add_far(r):
        return (acc[r] + work[list_ref[6, 0, r]]) * inv[r]

    group = [(dx, dc) for dx in range(4) for dc in range(2) if dx or dc]
    mine = pl.multiple_of((at["x"] * 2 + at["c"]) * 16, 16)

    def gram_copies(it, stage):
        copies = []
        if stage in (1, 2):
            axis = "yz"[stage - 1]
            for d in STEPS:
                copies.append(
                    pltpu.make_async_remote_copy(
                        gline.at[it, stage - 1, 0], gline.at[it, stage - 1, d],
                        gs.at[it, stage, d], gr.at[it, stage, d],
                        device_id=device(**{axis: d}), device_id_type=MESH,
                    )
                )
            return copies
        for dx, dc in group:
            by = {k: v for k, v in (("x", dx), ("c", dc)) if v}
            e = dx * 2 + dc
            if stage == 0:
                theirs = lax.rem(at["x"] + dx, 4) * 2 + lax.rem(at["c"] + dc, 2)
                src, dst = gsrc.at[it, pl.ds(pl.multiple_of(theirs * 16, 16), 16)], gpart.at[it, e]
            else:
                src = dst = gout.at[it, pl.ds(mine, 16)]
            copies.append(
                pltpu.make_async_remote_copy(
                    src, dst, gs.at[it, stage, e], gr.at[it, stage, e], device_id=device(**by), device_id_type=MESH
                )
            )
        return copies

    def gram_start(it, stage):
        for copy in gram_copies(it, stage):
            copy.start()

    def gram_finish(it, stage):
        for copy in gram_copies(it, stage):
            copy.wait()
        if stage == 0:
            total = gsrc[it, pl.ds(mine, 16)]
            for dx, dc in group:
                total = total + gpart[it, dx * 2 + dc]
        elif stage < 3:
            total = (gline[it, stage - 1, 0] + gline[it, stage - 1, 1]) + (gline[it, stage - 1, 2] + gline[it, stage - 1, 3])
        if stage < 2:
            gline[it, stage, 0] = total
        elif stage == 2:
            gout[it, pl.ds(mine, 16)] = total

    def local_gram(it):
        def add(r, total):
            a = acc[r]
            return total + lax.dot_general(
                a, a, (((0,), (0,)), ((), ())), precision=HIGH, preferred_element_type=F32
            )

        gsrc[it] = lax.fori_loop(0, ROWS, add, jnp.zeros((T, T), F32), unroll=8)

    root_total = jnp.sqrt(F32(ROWS * T * 128))

    def normalised(value):
        return root_total * lax.dot_general(
            value, factor[...], (((1,), (1,)), ((), ())), precision=HIGH, preferred_element_type=F32
        )

    for it in range(ITERS):

        def forward_start():
            for d in (1, 3):
                for i in range(3):
                    gather_copy(i, d, it).wait_recv()
                    forward_copy(i, d).start()

        def second_start(d1s, d2s):
            for pair in d2s:
                for d1 in d1s:
                    for i in range(3):
                        for d2 in pair:
                            second_copy(i, d2, d1).start()

        if it:
            pl.semaphore_wait(free_in, len(same_core))
            for d in (1, 3):
                for i in range(3):
                    gather_copy(i, d, it).start()
        else:
            forward_start()
        for i in range(3):
            select(i, 0, it)
        second_start((0,), ((2,), (1, 3)))
        if it:
            local_gram(0)
            gram_start(0, 0)
            lax.fori_loop(0, 5, home, 0)
            gram_finish(0, 0)
            gram_start(0, 1)
            forward_start()
        else:
            for d in STEPS:
                for i in range(3):
                    root_copy(i, d).wait_recv()
        for d in (1, 3):
            for i in range(3):
                select(i, d, it)
        second_start((1, 3), ((2,), (1, 3)))
        if it:
            gram_finish(0, 1)
            gram_start(0, 2)
            lax.fori_loop(5, 9, home, 0)
        for i in range(3):
            for d in (1, 3):
                forward_copy(i, d).wait_recv()
            select(i, 2, it)
        second_start((2,), ((2,), (1, 3)))
        if it:
            pl.semaphore_wait(free_out, len(all_peers))
        for i in range(3):
            third_start(i, 0)
            own_copy(i, 0).start()
        if it:
            gram_finish(0, 2)
            gram_start(0, 3)
        lax.fori_loop(9 if it else 0, ROWS, home, 0)
        for d2 in (2, 1, 3):
            for i in (1, 2, 0):
                for d1 in range(4):
                    second_copy(i, d2, d1).wait_recv()
                third_start(i, d2)
                own_copy(i, d2).start()
        if it:
            gram_finish(0, 3)
            inverse_factor(gout.at[0], factor)
        for i in range(3):
            for d in (1, 3):
                gather_copy(i, d, it).wait_send()
                forward_copy(i, d).wait_send()
            for d in STEPS:
                if it == 0:
                    root_copy(i, d).wait_send()
                for d1 in range(4):
                    second_copy(i, d, d1).wait_send()
            third_all(i).wait_send()
            for d2 in range(4):
                own_copy(i, d2).wait()
        if it == 0:
            for by in same_core:
                pl.semaphore_signal(free_in, inc=1, device_id=device(**by), device_id_type=MESH)
        for i in range(3):
            third_all(i).wait_recv()
        lax.fori_loop(0, 128 // FAR_STEP, far_products, jnp.zeros((T, T), F32))

        if it == 0:
            for by in all_peers:
                pl.semaphore_signal(free_out, inc=1, device_id=device(**by), device_id_type=MESH)

            def close(r, carry):
                image = add_far(r)
                acc[r] = image
                put(r, image * inv[r])
                return carry

            lax.fori_loop(0, ROWS, close, 0, unroll=4)
        else:

            def close_last(r, carry):
                acc[r] = normalised(add_far(r))
                return carry

            lax.fori_loop(0, ROWS, close_last, 0, unroll=8)
    local_gram(1)
    for stage in range(4):
        gram_start(1, stage)
        gram_finish(1, stage)
    inverse_factor(gout.at[1], factor)

    def finish(r, carry):
        out_ref[r] = normalised(acc[r])
        return carry

    lax.fori_loop(0, ROWS, finish, 0, unroll=8)


def per_device(tiles, tile_cols, tile_counts, block):
    smem, vmem = pl.BlockSpec(memory_space=pltpu.SMEM), pl.BlockSpec(memory_space=pltpu.VMEM)
    dma = pltpu.SemaphoreType.DMA
    out = pl.pallas_call(
        kernel,
        out_shape=jax.ShapeDtypeStruct((ROWS, T, T), F32),
        in_specs=[pl.BlockSpec(memory_space=pl.ANY), vmem, vmem, smem],
        out_specs=vmem,
        scratch_shapes=[
            pltpu.VMEM((ROWS, SLOTS, T, T), jnp.bfloat16),
            pltpu.VMEM((ROWS, SLOTS, T, T), jnp.bfloat16),
            pltpu.VMEM((128, T, T), F32),
            *[pltpu.VMEM((ROWS, n, T), F32) for n in PARTS for _ in range(3)],
            *[pltpu.VMEM((3, 4, 8, n, T), F32) for n in PARTS],
            *[pltpu.VMEM((4, 4, 8, n, T), F32) for n in PARTS],
            *[pltpu.VMEM((8, 16, n, T), F32) for n in PARTS],
            pltpu.VMEM((ROWS, T, T), F32),
            pltpu.VMEM((ROWS + 1, T, 2 * T), jnp.bfloat16),
            pltpu.VMEM((ROWS, T, T), F32),
            pltpu.VMEM((T, T), F32),
            *[pltpu.VMEM((4, n, T), F32) for n in PARTS],
            pltpu.VMEM((2, T, T), F32),
            pltpu.VMEM((2, 8, 16, T), F32),
            pltpu.VMEM((2, 2, 4, 16, T), F32),
            pltpu.VMEM((2, T, T), F32),
            pltpu.VMEM((T, T), F32),
            pltpu.VMEM((2, 4, 4, 4, 1, T), jnp.int32),
            pltpu.SMEM((2, 4, 4, 4, 1, T), jnp.int32),
            pltpu.VMEM((ROWS, T), jnp.int32),
            pltpu.VMEM((7, 1, T), jnp.int32),
            pltpu.SMEM((ROWS, T), jnp.int32),
            pltpu.SMEM((7, 1, T), jnp.int32),
            dma((ROWS,)),
            *[dma((3, 4)) for _ in range(6)],
            dma((3, 4, 4)),
            dma((3, 4, 4)),
            dma((3,)),
            dma((3,)),
            dma((3, 4)),
            dma((4, 4)),
            dma((4, 4)),
            dma,
            dma,
            dma,
            dma((2, 4, 8)),
            dma((2, 4, 8)),
            pltpu.SemaphoreType.REGULAR,
            pltpu.SemaphoreType.REGULAR,
        ],
        compiler_params=pltpu.CompilerParams(
            collective_id=0, has_side_effects=True, vmem_limit_bytes=63 * 2**20
        ),
    )(tiles, block.reshape(ROWS, T, T), tile_cols, tile_counts)
    return out.reshape(ROWS * T, T)


def solution(mesh):
    shard = ("row", "grp")
    return jax.shard_map(
        per_device,
        mesh=mesh,
        in_specs=(P(shard, None, None, None), P(shard, None), P(shard), P(shard, None)),
        out_specs=P(shard, None),
        check_vma=False,
    )
```
